256 devices in a mesh: mass: 32 (over z, x), rep: 8 (over y, core).
Axes of the slice: x: 4, y: 4, z: 8, core: 2. Of those that a mesh axis runs over, the one named last changes fastest.
Arguments:
- queries: bfloat16 [32768, 4096], P(('mass', 'rep'))
- library: bfloat16 [49152, 4096], P(('mass', 'rep'))
- windows: int32 [4096, 4], P(('mass', 'rep')), may hold values from 0 to 31, all different within a row; in each aligned block of 16 rows (0 to 15, 16 to 31, ...) at most 3 rows name the same one
Outputs:
- top_scores: float32 [32768, 128], P(('mass', 'rep'))
The draws below stay inside these ranges and needn't reach their ends.
Inputs may be any that keep to these rules, and one draw needn't show every extreme that they name: `windows`: each row names 4 different shards. Among the 16 rows of one device no shard is named more than 3 times, a bound that some block reaches.
All inputs are finite; a program needn't handle non-finite values.
Results may differ from the reference program's by a relative error of at most 0.0015.
Values may be sent and summed in bfloat16 or wider, within the bound.
A program may use at most 128 MiB of HBM per device.

```python
import math
import jax
import jax.numpy as jnp
import numpy as np
from jax import lax

BINS = 4096
QB = 8
BPD = 16
TOPW = 4
K = 128
CAP = 3
BLOCKS = 4096
QUERIES = 32768
LIBRARY = 49152
SHARD = 1536
N_MASS = 32


def scaled_rows(noise, key, row_total, spread):
    row_key, col_key = jax.random.split(key)
    row_scale = jnp.exp(jax.random.uniform(row_key, (row_total, 1), jnp.float32) * jnp.log(spread))
    col_scale = jnp.exp(jax.random.uniform(col_key, (1, BINS), jnp.float32) * jnp.log(10.0))
    return noise * row_scale * col_scale


def spectra(key, row_total):
    noise_key, scale_key = jax.random.split(key)
    noise = jnp.clip(jax.random.normal(noise_key, (row_total, BINS), jnp.float32), -4.0, 4.0)
    spread = 10.0
    return scaled_rows(noise, scale_key, row_total, spread).astype(jnp.bfloat16)


def draw_queries(key, part):
    key = jax.random.fold_in(key, 11)
    return spectra(key, QUERIES)


def draw_library(key, part):
    key = jax.random.fold_in(key, 23)
    return spectra(key, LIBRARY)


def shared_out(rng, own, number, rows, count, top, bound, slope):
    ranking = jax.random.permutation(rng, count)
    crowded, usual = shares(count, rows * top, bound, slope, True), shares(count, rows * top, bound, slope, False)
    places = jnp.arange(count)

    def named(tallies, rotation):
        used = int((tallies > 0).sum())
        fixed = max(1, used // 4)
        shifted = fixed + (places - fixed + rotation * (used - fixed)) % max(1, count - fixed)
        return jnp.zeros((count,), jnp.int32).at[ranking[jnp.where(places < fixed, places, shifted)]].set(jnp.asarray(tallies, jnp.int32))

    tallies = jnp.where(number % 4 == 0, named(crowded, number // 4), named(usual, number - number // 4 - 1))
    mixed = jax.random.permutation(jax.random.fold_in(own, 3), count)
    donor, taker = mixed[0:count // 2 * 2:2], mixed[1:count // 2 * 2:2]
    margin = jnp.minimum(tallies[donor] - 1, bound - tallies[taker]) // 2
    margin = jnp.where((donor == ranking[0]) | (taker == ranking[0]) | (tallies[taker] == 0), 0, jnp.maximum(margin, 0))
    shifted = jax.random.randint(jax.random.fold_in(own, 4), (count // 2,), 0, 1 << 20) % (margin + 1)
    tallies = tallies.at[donor].add(-shifted).at[taker].add(shifted)
    labels = jnp.searchsorted(jnp.cumsum(tallies), jnp.arange(rows * top), side="right").astype(jnp.int32)
    listing = labels.reshape(top, rows).T
    listing = listing[jax.random.permutation(jax.random.fold_in(own, 1), rows)]
    rotation = jax.random.randint(jax.random.fold_in(own, 2), (rows, 1), 0, top)
    return jnp.take_along_axis(listing, (jnp.arange(top)[None, :] + rotation) % top, axis=1)


def shares(count, total, reach, lean, full):
    weights = [(1 << 20) // math.isqrt(grade ** lean) + 1 for grade in range(1, count + 1)]
    largest = reach if full else min(reach, max(-(-total // count), total * weights[0] // sum(weights)))
    least = 1 if total - largest >= count - 1 else 0
    counts, surplus = [largest] + [least] * (count - 1), total - largest - least * (count - 1)
    while surplus > 0:
        movable = [i for i in range(1, count) if counts[i] < largest] or [i for i in range(1, count) if counts[i] < reach]
        mass, remaining = sum([weights[i] for i in movable]), surplus
        for i in movable:
            addition = min(reach - counts[i], max(1, remaining * weights[i] // mass), surplus)
            counts[i] = counts[i] + addition
            surplus = surplus - addition
    return np.array(counts)


def setup_inputs(seed: int = 0) -> dict:
    splits = jax.random.split(jax.random.key(seed), 4)
    queries = draw_queries(jax.random.fold_in(splits[3], 71), 0)
    library = draw_library(jax.random.fold_in(splits[3], 71), 0)
    windows_keys = jax.random.split(jax.random.fold_in(splits[2], 1), BLOCKS // BPD)
    windows_turns = jax.random.permutation(jax.random.fold_in(splits[2], 3), BLOCKS // BPD)
    windows = jax.vmap(lambda own, number: shared_out(jax.random.fold_in(splits[2], 2), own, number, BPD, N_MASS, TOPW, CAP, 2))(windows_keys, windows_turns).reshape((BLOCKS, TOPW))
    return {"queries": queries, "library": library, "windows": windows}


epsilon = 1e-06

def unit_rows(values):
    widened = values.astype(jnp.float32)
    inverse = lax.rsqrt(lax.optimization_barrier(jnp.mean(widened * widened, axis=-1, keepdims=True)) + epsilon)
    return (widened * inverse).astype(jnp.bfloat16)

def reference(queries, library, windows):
    query_unit = unit_rows(queries).reshape(BLOCKS, QB, BINS)
    library_unit = unit_rows(library)
    score_scale = 1.0 / math.sqrt(BINS)

    def search(item):
        block_rows, shard_list = item
        pieces = []
        for visit in range(TOPW):
            first_row = shard_list[visit].astype(jnp.int32) * SHARD
            shard_rows = lax.dynamic_slice_in_dim(library_unit, first_row, SHARD, 0)
            pieces.append(jnp.dot(block_rows, shard_rows.T, preferred_element_type=jnp.float32) * score_scale)
        return lax.top_k(jnp.concatenate(pieces, axis=1), K)[0]
    best_scores = lax.map(search, (query_unit, windows))
    return best_scores.reshape(QUERIES, K)
```

```python
import math

import jax
import jax.numpy as jnp
from jax import lax
from jax.experimental import pallas as pl
from jax.experimental.pallas import tpu as pltpu
from jax.sharding import PartitionSpec as P

MESH = pl.DeviceIdType.MESH
NZ, NX, NY = 8, 4, 4
BINS = 4096
HALF, QUARTER = BINS // 2, BINS // 4
QB = 8
BLOCKS = 16
TOPW = 4
CAP = 3
K = 128
ENTRIES = 192
SHARD = 1536
SLOT = 2 * QB
UNIT = CAP * SLOT
SLOTS = NX * CAP * QB
epsilon = 1e-06

OFFSET = (0, -1, 1, -2, 2, -3, 3, -4)
PIECES = [(s, a, b, p) for s, a, b in ((1, 0, 1), (-1, 0, 2), (1, 1, 3), (-1, 2, 4), (1, 3, 5)) for p in (0, 1)]
LAST = {10: (-1, 4, 6, 0), 11: (-1, 4, 6, 1), 12: (1, 5, 7, 0), 13: (1, 5, 7, 1)}
CODES = ((1, 1, 1), (-1, -1, 2), (2, 2, 3), (-2, -2, 4), (3, 3, 5), (-2, -3, 6), (3, 4, 7))


def at_index(v, i, axis):
    return lax.index_in_dim(v, i, axis, keepdims=False)


def paired(a, b, axis, up):
    hi, lo = jnp.maximum(a, b), jnp.minimum(a, b)
    return jnp.stack([lo, hi] if up else [hi, lo], axis=axis)


def clean(v, top, low, up=False):
    shape = v.shape
    s = top
    while s >= low:
        w = v.reshape((shape[0] // (2 * s), 2, s) + shape[1:])
        v = paired(at_index(w, 0, 1), at_index(w, 1, 1), 1, up).reshape(shape)
        s //= 2
    return v


def batcher(v):
    n = v.shape[0]
    shape = v.shape
    p = 1
    while p < n:
        k = p
        while k >= 1:
            w = v.reshape((n // (2 * p), 2 * p // k, k) + shape[1:])
            if k == p:
                w = paired(at_index(w, 0, 1), at_index(w, 1, 1), 1, False)
            else:
                c = 2 * p // k
                mid = lax.slice_in_dim(w, 1, c - 1, axis=1)
                mid = mid.reshape((n // (2 * p), (c - 2) // 2, 2, k) + shape[1:])
                mid = paired(at_index(mid, 0, 2), at_index(mid, 1, 2), 2, False)
                mid = mid.reshape((n // (2 * p), c - 2, k) + shape[1:])
                w = jnp.concatenate([lax.slice_in_dim(w, 0, 1, axis=1), mid, lax.slice_in_dim(w, c - 1, c, axis=1)], axis=1)
            v = w.reshape(shape)
            k //= 2
        p *= 2
    return v


def backwards(v):
    n = v.shape[0]
    return jnp.concatenate([lax.slice_in_dim(v, n - 1 - i, n - i, axis=0) for i in range(n)], axis=0)


def repeat(count, body, unroll=True):
    def step(i, carry):
        body(i)
        return carry
    lax.fori_loop(0, count, step, 0, unroll=unroll)


def coarse(ref, base, n, top, low, i, width, up=False):
    v = jnp.stack([ref[pl.ds(base + n * j + i, width)] for j in range(8)], axis=0)
    v = clean(v, top, low, up)
    for j in range(8):
        ref[pl.ds(base + n * j + i, width)] = at_index(v, j, 0)


def fine(ref, base, n, groups, i, up=False):
    at = pl.ds(base + i * n * groups, n * groups)
    ref[at] = clean(ref[at], n // 2, 1, up)


def across(ref, shift):
    def body(i):
        i = i * 4
        a = jnp.stack([ref[pl.ds(16 * j + i, 4)] for j in range(8)], axis=0)
        r = jnp.stack([ref[pl.ds(16 * j + 12 - i, 4)] for j in range(8)], axis=0)
        flat = (32, 8, 128)
        ra = backwards(r.reshape(flat))
        rr = backwards(a.reshape(flat))
        a = jnp.maximum(a.reshape(flat), pltpu.roll(ra, shift, 1)).reshape(8, 4, 8, 128)
        r = jnp.maximum(r.reshape(flat), pltpu.roll(rr, shift, 1)).reshape(8, 4, 8, 128)
        a, r = clean(a, 4, 1), clean(r, 4, 1)
        for j in range(8):
            ref[pl.ds(16 * j + i, 4)] = at_index(a, j, 0)
            ref[pl.ds(16 * j + 12 - i, 4)] = at_index(r, j, 0)
    repeat(2, body)


def collect(ref, o_ref):
    own = lax.broadcasted_iota(jnp.int32, (1, 8, 8, 128), 1) == lax.broadcasted_iota(jnp.int32, (1, 8, 8, 128), 2)
    def body(g):
        v = clean(ref[pl.ds(g * 32, 32)], 8, 1).reshape(4, 8, 8, 128)
        o_ref[pl.ds(pl.multiple_of(g * 32, 32), 32), :] = jnp.sum(jnp.where(own, v, 0.0), axis=1).reshape(32, 128)
    repeat(4, body)


def top_rows(ref, o_ref):
    def sort32(c):
        for up in (0, 1):
            at = pl.ds((c * 2 + up) * 32, 32)
            v = batcher(ref[at])
            ref[at] = backwards(v) if up else v
    repeat(3, sort32, False)
    for c in range(3):
        repeat(2, lambda i: coarse(ref, c * 64, 8, 4, 1, i * 4, 4, c > 0))
        repeat(2, lambda i: fine(ref, c * 64, 8, 4, i, c > 0))
    def third(i):
        i = i * 4
        v = [ref[pl.ds(16 * j + i, 4)] for j in range(8)]
        for j in range(4, 8):
            v[j] = jnp.maximum(v[j], ref[pl.ds(16 * j + 64 + i, 4)])
        v = clean(jnp.stack(v, axis=0), 4, 1)
        for j in range(8):
            ref[pl.ds(16 * j + i, 4)] = at_index(v, j, 0)
    repeat(4, lambda i: coarse(ref, 0, 16, 4, 1, i * 4, 4))
    repeat(4, lambda i: fine(ref, 0, 16, 2, i))
    repeat(4, third)
    repeat(4, lambda i: fine(ref, 0, 16, 2, i))
    for shift in (4, 2, 1):
        across(ref, shift)
        if shift != 1:
            repeat(4, lambda i: fine(ref, 0, 16, 2, i))
    collect(ref, o_ref)


def kernel(
    q_hbm, l_hbm, w_ref, o_ref,
    q_in, l_in, chunk, packed, arrived, rows, lib, scores, best, outgoing, incoming, code_own, code_in, slot_of, lists, mixed,
    load_sem, zs, zr, xs, xr, cs, cr, ys, yr, ks, kr, rs, rr,
):
    m, r = lax.axis_index("mass"), lax.axis_index("rep")
    z, x, y, c = m // NX, m % NX, r // 2, r % 2
    sign = 2 * c - 1

    def mass_at(dz, dx):
        return (z + dz * sign + NZ) % NZ * NX + (x + dx) % NX

    def remote(src, dst, send, recv, device):
        return pltpu.make_async_remote_copy(
            src_ref=src, dst_ref=dst, send_sem=send, recv_sem=recv, device_id=device, device_id_type=MESH
        )

    def y_rep(dy, core):
        return (y + dy * sign + NY) % NY * 2 + core

    load_q = pltpu.make_async_copy(q_hbm, q_in, load_sem.at[0])
    load_l = pltpu.make_async_copy(l_hbm, l_in, load_sem.at[1])
    load_q.start()
    load_l.start()

    barrier = pltpu.get_barrier_semaphore()

    def greet(i):
        pl.semaphore_signal(barrier, inc=1, device_id=((m + i + 1) % (NZ * NX), r), device_id_type=MESH)

    repeat(NZ * NX - 1, greet, False)
    for dy in (1, 2, 3):
        pl.semaphore_signal(barrier, inc=1, device_id=(m, y_rep(dy, c)), device_id_type=MESH)
    pl.semaphore_signal(barrier, inc=1, device_id=(m, y * 2 + 1 - c), device_id_type=MESH)

    def unit(values):
        widened = values.astype(jnp.float32)
        inverse = lax.rsqrt(jnp.mean(widened * widened, axis=-1, keepdims=True) + epsilon)
        return widened * inverse

    load_q.wait()

    def own_rows(i):
        two = unit(q_in[pl.ds(pl.multiple_of(i * 16, 16), 16), :])
        for b in (0, 1):
            u = two[b * 8 : b * 8 + 8]
            for p in (0, 1):
                halves = [u[:, p * HALF + h * QUARTER : p * HALF + (h + 1) * QUARTER] for h in (0, 1)]
                at = pl.ds(pl.multiple_of((i * 2 + b) * SLOT, SLOT), SLOT)
                chunk[0, p, at, :] = jnp.concatenate(halves, axis=0).astype(jnp.bfloat16)

    repeat(8, own_rows, False)

    lane_block = lax.broadcasted_iota(jnp.int32, (1, 256), 1) // SLOT
    shard_id = lax.broadcasted_iota(jnp.int32, (64, 256), 0)
    shard_id = shard_id // 8 * NX + shard_id % NX
    hit = jnp.zeros((64, 256), jnp.float32)
    for v in range(TOPW):
        named = jnp.zeros((1, 256), jnp.int32)
        for b in range(BLOCKS):
            named = jnp.where(lane_block == b, w_ref[b, v], named)
        hit = jnp.where(shard_id == named, 1.0, hit)
    before = lax.broadcasted_iota(jnp.int32, (256, 256), 0)
    after = lax.broadcasted_iota(jnp.int32, (256, 256), 1) // SLOT
    earlier = jnp.where((before // SLOT < after) & (before % SLOT == 0), 1.0, 0.0).astype(jnp.bfloat16)
    count = jnp.dot(hit.astype(jnp.bfloat16), earlier, preferred_element_type=jnp.float32)
    code = jnp.where(hit > 0.5, count, -1.0)
    for plane in range(NZ):
        code_own[plane] = code[plane * 8 : plane * 8 + 8]

    pl.semaphore_wait(barrier, NZ * NX - 1 + NY - 1 + 1)

    codes = {}
    for dz, dp, k in CODES:
        codes[k] = remote(
            code_own.at[(z + dp * sign + NZ) % NZ], code_in.at[k], cs.at[k], cr.at[k], (mass_at(dz, 0), r)
        )
        codes[k].start()

    ring = []
    for n, (s, a, b, p) in enumerate(PIECES):
        ring.append(remote(chunk.at[a, p], chunk.at[b, p], zs.at[n], zr.at[n], (mass_at(s, 0), r)))
    for n in (0, 1):
        ring[n].start()

    load_l.wait()

    def own_entries(i):
        at = pl.multiple_of(i * 16, 16)
        lib[pl.ds(pl.multiple_of(r * ENTRIES + at, 16), 16), :] = unit(l_in[pl.ds(at, 16), :]).astype(jnp.bfloat16)

    repeat(ENTRIES // 16, own_entries, False)

    def entries(rep, part=None):
        first, size = (0, ENTRIES) if part is None else (part * (ENTRIES // 2), ENTRIES // 2)
        return lib.at[pl.ds(pl.multiple_of(rep * ENTRIES + first, 16), size)]

    def along_y(n, rep, dy, part=None):
        return remote(entries(rep, part), entries(rep, part), ys.at[n], yr.at[n], (m, y_rep(dy, c)))

    def to_sibling(n, rep):
        return remote(entries(rep), entries(rep), ks.at[n], kr.at[n], (m, y * 2 + 1 - c))

    lib_y = [along_y(0, r, 1), along_y(1, r, -1), along_y(2, y_rep(-1, c), 1, 0), along_y(3, y_rep(1, c), -1, 1)]
    lib_c = [to_sibling(n, y_rep(dy, c)) for n, dy in enumerate((0, -1, 1, 2))]
    lib_y[0].start()
    lib_c[0].start()

    diagonal = lax.broadcasted_iota(jnp.int32, (SLOT, 256), 1) % SLOT == lax.broadcasted_iota(jnp.int32, (SLOT, 256), 0)

    def pick(k, p, held):
        parts = []
        for d in range(NX):
            at = pl.ds((x + d) % NX, 1)
            line = code_own[z, at, :] if k == 0 else code_in[k, at, :]
            for slot in range(CAP):
                parts.append(jnp.where(diagonal & (line == float(slot)), 1.0, 0.0))
        select = jnp.concatenate(parts, axis=0).astype(jnp.bfloat16)
        for t in range(QUARTER // 256):
            at = pl.ds(t * 256, 256)
            out = jnp.dot(select, chunk[held, p, :, at], preferred_element_type=jnp.float32).astype(jnp.bfloat16)
            for d in range(NX):
                part = out[d * UNIT : (d + 1) * UNIT]
                if d == 0 and k < 6:
                    arrived[k, p, 0, :, at] = part
                else:
                    packed[k, p, d, :, at] = part

    hops = {}
    for k in range(8):
        dz = {6: -1, 7: 1}.get(k, 0)
        for p in (0, 1):
            for d in range(NX):
                if d or k >= 6:
                    hops[k, p, d] = remote(
                        packed.at[k, p, d], arrived.at[k, p, d], xs.at[k, p, d], xr.at[k, p, d], (mass_at(dz, d), r)
                    )

    def send(k, p):
        for d in range(NX):
            if (k, p, d) in hops:
                hops[k, p, d].start()

    def unpack(k):
        for p in (0, 1):
            for d in range(NX):
                if (k, p, d) in hops:
                    hops[k, p, d].wait_recv()
        for p in (0, 1):
            for j in range(NX * CAP // 2):
                two = []
                for s in (2 * j, 2 * j + 1):
                    at = pl.ds(s % CAP * SLOT, SLOT)
                    two.append(arrived[k, p, s // CAP, at, :].astype(jnp.float32))
                for h in (0, 1):
                    block = jnp.concatenate([v[h * 8 : h * 8 + 8] for v in two], axis=0).astype(jnp.bfloat16)
                    first = p * HALF + h * QUARTER
                    rows[k * SLOTS + j * 16 : k * SLOTS + j * 16 + 16, first : first + QUARTER] = block

    def score(group, groups, rep):
        at = pl.ds(pl.multiple_of(rep * ENTRIES, 16), ENTRIES)
        out = lax.dot_general(
            lib[at, :],
            rows[group * 128 : (group + groups) * 128, :],
            (((1,), (1,)), ((), ())),
            preferred_element_type=jnp.float32,
        )
        for g in range(groups):
            part = out[:, g * 128 : g * 128 + 128].reshape(ENTRIES // 8, 8, 128)
            scores[group + g, pl.ds(rep * (ENTRIES // 8), ENTRIES // 8)] = part

    returns = {}
    for k in range(8):
        for d in range(NX):
            if k or d:
                at = pl.ds(k * SLOTS + d * CAP * QB, CAP * QB)
                returns[k, d] = remote(
                    outgoing.at[at], incoming.at[m], rs.at[k, d], rr.at[k, d], (mass_at(OFFSET[k], NX - d), r)
                )

    def choose(group):
        top_rows(scores.at[group], best)
        outgoing[group * 128 : group * 128 + 128, :] = best[...].T

    def give_back(k):
        for d in range(NX):
            if k or d:
                returns[k, d].start()
            else:
                incoming[m] = outgoing[0 : CAP * QB, :]

    pick(0, 0, 0)
    send(0, 0)
    pick(0, 1, 0)
    send(0, 1)

    for b in range(BLOCKS):
        for v in range(TOPW):
            shard = w_ref[b, v]
            line = code_own[shard // NX, pl.ds(shard % NX, 1), :]
            slot_of[b, v] = jnp.broadcast_to(line[:, b * SLOT : b * SLOT + 1], (8, 128))

    quarter = [
        (r, y * 2 + 1 - c),
        (y_rep(-1, c), y_rep(1, 1 - c)),
        (y_rep(1, c), y_rep(-1, 1 - c)),
        (y_rep(2, c), y_rep(2, 1 - c)),
    ]

    def score_quarters(group, groups, which):
        for i in which:
            for rep in quarter[i]:
                score(group, groups, rep)

    def score_all(group, groups):
        repeat(2 * NY, lambda rep: score(group, groups, rep), False)

    for n in range(14):
        if n < 10:
            ring[n].wait_send()
        else:
            k, p = LAST[n][2], LAST[n][3]
            for d in range(NX):
                hops[k, p, d].wait_send()
        if n + 2 < 10:
            ring[n + 2].start()
        elif n + 2 < 14:
            send(LAST[n + 2][2], LAST[n + 2][3])
        if n < 10:
            ring[n].wait_recv()
            b, p = PIECES[n][2], PIECES[n][3]
            if p == 0:
                codes[b].wait_recv()
            pick(b, p, b)
            send(b, p)
            if b in (4, 5):
                if p == 0:
                    codes[b + 2].wait_recv()
                pick(b + 2, p, b)
        if n == 2:
            lib_y[0].wait_send()
            lib_y[1].start()
            unpack(0)
            unpack(1)
        elif n == 3:
            lib_y[0].wait_recv()
            lib_c[1].start()
            lib_c[0].wait_recv()
        elif n == 4:
            unpack(2)
            lib_c[1].wait_recv()
            score_quarters(0, 2, (0, 1))
        elif n == 5:
            lib_y[1].wait_send()
            lib_y[2].start()
        elif n == 6:
            lib_y[1].wait_recv()
            lib_y[3].start()
            lib_c[2].start()
            unpack(3)
            score_quarters(2, 1, (0, 1))
        elif n == 7:
            lib_c[2].wait_recv()
            score_quarters(0, 2, (2,))
            score_quarters(2, 1, (2,))
        elif n == 8:
            unpack(4)
        elif n == 9:
            lib_y[2].wait_recv()
            lib_y[3].wait_recv()
            lib_c[3].start()
            lib_c[3].wait_recv()
            score_quarters(0, 2, (3,))
            choose(0)
            give_back(0)
            choose(1)
            give_back(1)
        elif n == 10:
            unpack(5)
            score_quarters(2, 1, (3,))
            choose(2)
            give_back(2)
            give_back(3)
            score_all(3, 1)
        elif n == 11:
            choose(3)
            give_back(4)
        elif n == 12:
            unpack(6)
            score_all(4, 1)
            choose(4)
            give_back(5)
    unpack(7)
    score_all(5, 1)
    choose(5)
    give_back(6)
    give_back(7)

    for k, d in returns:
        returns[k, d].wait_recv()

    def fetch(b):
        for v in range(TOPW):
            shard, slot = w_ref[b, v], slot_of[b, v]
            found = [incoming[shard, i * QB : i * QB + QB, :] for i in range(CAP)]
            found = jnp.where(slot < 0.5, found[0], jnp.where(slot < 1.5, found[1], found[2]))
            lists[v, pl.ds(pl.multiple_of(b * QB, QB), QB), :] = found

    repeat(BLOCKS, fetch, 4)
    for v in range(TOPW):
        lists[v] = lists[v].T
    sub = lax.broadcasted_iota(jnp.int32, (8, 128), 0) % TOPW

    def mix(i):
        line = [lists[v, pl.ds(i, 1), :] for v in range(TOPW)]
        mixed[i] = jnp.where(sub == 0, line[0], jnp.where(sub == 1, line[1], jnp.where(sub == 2, line[2], line[3])))

    repeat(K, mix, 16)
    across(mixed, 2)
    repeat(4, lambda i: fine(mixed, 0, 16, 2, i))
    across(mixed, 1)
    collect(mixed, best)
    o_ref[...] = best[...].T

    for copy in codes.values():
        copy.wait_send()
    for k in range(6):
        for p in (0, 1):
            for d in range(1, NX):
                hops[k, p, d].wait_send()
    for n in (2, 3):
        lib_y[n].wait_send()
    for copy in lib_c:
        copy.wait_send()
    for copy in returns.values():
        copy.wait_send()


def on_device(queries, library, windows):
    bf16, f32, dma = jnp.bfloat16, jnp.float32, pltpu.SemaphoreType.DMA
    scores = pl.pallas_call(
        kernel,
        out_shape=jax.ShapeDtypeStruct((BLOCKS * QB, K), f32),
        in_specs=[
            pl.BlockSpec(memory_space=pl.ANY),
            pl.BlockSpec(memory_space=pl.ANY),
            pl.BlockSpec(memory_space=pltpu.SMEM),
        ],
        out_specs=pl.BlockSpec(memory_space=pltpu.VMEM),
        scratch_shapes=[
            pltpu.VMEM((BLOCKS * QB, BINS), bf16),
            pltpu.VMEM((ENTRIES, BINS), bf16),
            pltpu.VMEM((6, 2, BLOCKS * SLOT, QUARTER), bf16),
            pltpu.VMEM((8, 2, NX, UNIT, QUARTER), bf16),
            pltpu.VMEM((8, 2, NX, UNIT, QUARTER), bf16),
            pltpu.VMEM((8 * SLOTS, BINS), bf16),
            pltpu.VMEM((SHARD, BINS), bf16),
            pltpu.VMEM((6, SHARD // 8, 8, 128), f32),
            pltpu.VMEM((128, 128), f32),
            pltpu.VMEM((8 * SLOTS, K), f32),
            pltpu.VMEM((NZ * NX, CAP * QB, K), f32),
            pltpu.VMEM((NZ, 8, 256), f32),
            pltpu.VMEM((8, 8, 256), f32),
            pltpu.VMEM((BLOCKS, TOPW, 8, 128), f32),
            pltpu.VMEM((TOPW, 128, K), f32),
            pltpu.VMEM((K, 8, 128), f32),
            dma((2,)),
            dma((10,)),
            dma((10,)),
            dma((8, 2, NX)),
            dma((8, 2, NX)),
            dma((8,)),
            dma((8,)),
            dma((4,)),
            dma((4,)),
            dma((4,)),
            dma((4,)),
            dma((8, NX)),
            dma((8, NX)),
        ],
        compiler_params=pltpu.CompilerParams(
            collective_id=0, has_side_effects=True, vmem_limit_bytes=60 * 2**20
        ),
    )(queries, library, windows)
    return scores * (1.0 / math.sqrt(BINS))


def solution(mesh):
    placed = (P(("mass", "rep"), None), P(("mass", "rep"), None), P(("mass", "rep"), None))
    return jax.shard_map(
        on_device, mesh=mesh, in_specs=placed, out_specs=P(("mass", "rep"), None), check_vma=False
    )
```

```python
import math

import jax
import jax.numpy as jnp
from jax import lax
from jax.experimental import pallas as pl
from jax.experimental.pallas import tpu as pltpu
from jax.sharding import PartitionSpec as P

MESH = pl.DeviceIdType.MESH
NZ, NX, NY = 8, 4, 4
BINS = 4096
HALF, QUARTER = BINS // 2, BINS // 4
QB = 8
BLOCKS = 16
TOPW = 4
CAP = 3
K = 128
ENTRIES = 192
SHARD = 1536
SLOT = 2 * QB
UNIT = CAP * SLOT
SLOTS = NX * CAP * QB
epsilon = 1e-06

OFFSET = (0, -1, 1, -2, 2, -3, 3, -4)
PIECES = [(s, a, b, p) for s, a, b in ((1, 0, 1), (-1, 0, 2), (1, 1, 3), (-1, 2, 4), (1, 3, 5)) for p in (0, 1)]
LAST = {10: (-1, 4, 6, 0), 11: (-1, 4, 6, 1), 12: (1, 5, 7, 0), 13: (1, 5, 7, 1)}
CODES = ((1, 1, 1), (-1, -1, 2), (2, 2, 3), (-2, -2, 4), (3, 3, 5), (-2, -3, 6), (3, 4, 7))


def at_index(v, i, axis):
    return lax.index_in_dim(v, i, axis, keepdims=False)


def paired(a, b, axis, up):
    hi, lo = jnp.maximum(a, b), jnp.minimum(a, b)
    return jnp.stack([lo, hi] if up else [hi, lo], axis=axis)


def clean(v, top, low, up=False):
    shape = v.shape
    s = top
    while s >= low:
        w = v.reshape((shape[0] // (2 * s), 2, s) + shape[1:])
        v = paired(at_index(w, 0, 1), at_index(w, 1, 1), 1, up).reshape(shape)
        s //= 2
    return v


def batcher(v):
    n = v.shape[0]
    shape = v.shape
    p = 1
    while p < n:
        k = p
        while k >= 1:
            w = v.reshape((n // (2 * p), 2 * p // k, k) + shape[1:])
            if k == p:
                w = paired(at_index(w, 0, 1), at_index(w, 1, 1), 1, False)
            else:
                c = 2 * p // k
                mid = lax.slice_in_dim(w, 1, c - 1, axis=1)
                mid = mid.reshape((n // (2 * p), (c - 2) // 2, 2, k) + shape[1:])
                mid = paired(at_index(mid, 0, 2), at_index(mid, 1, 2), 2, False)
                mid = mid.reshape((n // (2 * p), c - 2, k) + shape[1:])
                w = jnp.concatenate([lax.slice_in_dim(w, 0, 1, axis=1), mid, lax.slice_in_dim(w, c - 1, c, axis=1)], axis=1)
            v = w.reshape(shape)
            k //= 2
        p *= 2
    return v


def backwards(v):
    n = v.shape[0]
    return jnp.concatenate([lax.slice_in_dim(v, n - 1 - i, n - i, axis=0) for i in range(n)], axis=0)


def repeat(count, body, unroll=True):
    def step(i, carry):
        body(i)
        return carry
    lax.fori_loop(0, count, step, 0, unroll=unroll)


def coarse(ref, base, n, top, low, i, width, up=False):
    v = jnp.stack([ref[pl.ds(base + n * j + i, width)] for j in range(8)], axis=0)
    v = clean(v, top, low, up)
    for j in range(8):
        ref[pl.ds(base + n * j + i, width)] = at_index(v, j, 0)


def fine(ref, base, n, groups, i, up=False):
    at = pl.ds(base + i * n * groups, n * groups)
    ref[at] = clean(ref[at], n // 2, 1, up)


def across(ref, shift):
    def body(i):
        i = i * 4
        a = jnp.stack([ref[pl.ds(16 * j + i, 4)] for j in range(8)], axis=0)
        r = jnp.stack([ref[pl.ds(16 * j + 12 - i, 4)] for j in range(8)], axis=0)
        flat = (32, 8, 128)
        ra = backwards(r.reshape(flat))
        rr = backwards(a.reshape(flat))
        a = jnp.maximum(a.reshape(flat), pltpu.roll(ra, shift, 1)).reshape(8, 4, 8, 128)
        r = jnp.maximum(r.reshape(flat), pltpu.roll(rr, shift, 1)).reshape(8, 4, 8, 128)
        a, r = clean(a, 4, 1), clean(r, 4, 1)
        for j in range(8):
            ref[pl.ds(16 * j + i, 4)] = at_index(a, j, 0)
            ref[pl.ds(16 * j + 12 - i, 4)] = at_index(r, j, 0)
    repeat(2, body)


def collect(ref, o_ref):
    own = lax.broadcasted_iota(jnp.int32, (1, 8, 8, 128), 1) == lax.broadcasted_iota(jnp.int32, (1, 8, 8, 128), 2)
    def body(g):
        v = clean(ref[pl.ds(g * 32, 32)], 8, 1).reshape(4, 8, 8, 128)
        o_ref[pl.ds(pl.multiple_of(g * 32, 32), 32), :] = jnp.sum(jnp.where(own, v, 0.0), axis=1).reshape(32, 128)
    repeat(4, body)


def sort_part(ref, c):
    def sort32(up):
        at = pl.ds(c * 64 + up * 32, 32)
        v = batcher(ref[at])
        ref[at] = backwards(v) if up else v

    for up in (0, 1):
        sort32(up)
    repeat(2, lambda i: coarse(ref, c * 64, 8, 4, 1, i * 4, 4, c > 0))
    repeat(2, lambda i: fine(ref, c * 64, 8, 4, i, c > 0))


def begin_rows(ref):
    for c in (0, 1):
        sort_part(ref, c)
    repeat(4, lambda i: coarse(ref, 0, 16, 4, 1, i * 4, 4))
    repeat(4, lambda i: fine(ref, 0, 16, 2, i))


def end_rows(ref, o_ref):
    def third(i):
        i = i * 4
        v = [ref[pl.ds(16 * j + i, 4)] for j in range(8)]
        for j in range(4, 8):
            v[j] = jnp.maximum(v[j], ref[pl.ds(16 * j + 64 + i, 4)])
        v = clean(jnp.stack(v, axis=0), 4, 1)
        for j in range(8):
            ref[pl.ds(16 * j + i, 4)] = at_index(v, j, 0)

    sort_part(ref, 2)
    repeat(4, third)
    repeat(4, lambda i: fine(ref, 0, 16, 2, i))
    for shift in (4, 2, 1):
        across(ref, shift)
        if shift != 1:
            repeat(4, lambda i: fine(ref, 0, 16, 2, i))
    collect(ref, o_ref)


def kernel(
    q_hbm, l_hbm, w_ref, o_ref,
    q_in, l_in, chunk, packed, arrived, rows, lib, scores, best, outgoing, incoming, code_own, code_in, slot_of, lists, mixed,
    load_sem, zs, zr, xs, xr, cs, cr, ys, yr, ks, kr, rs, rr,
):
    m, r = lax.axis_index("mass"), lax.axis_index("rep")
    z, x, y, c = m // NX, m % NX, r // 2, r % 2
    sign = 2 * c - 1

    def mass_at(dz, dx):
        return (z + dz * sign + NZ) % NZ * NX + (x + dx) % NX

    def remote(src, dst, send, recv, device):
        return pltpu.make_async_remote_copy(
            src_ref=src, dst_ref=dst, send_sem=send, recv_sem=recv, device_id=device, device_id_type=MESH
        )

    def y_rep(dy, core):
        return (y + dy * sign + NY) % NY * 2 + core

    load_q = pltpu.make_async_copy(q_hbm, q_in, load_sem.at[0])
    load_l = pltpu.make_async_copy(l_hbm, l_in, load_sem.at[1])
    load_q.start()
    load_l.start()

    barrier = pltpu.get_barrier_semaphore()

    for dz in (1, 2, 3, 5, 6, 7):
        pl.semaphore_signal(barrier, inc=1, device_id=((z + dz) % NZ * NX + x, r), device_id_type=MESH)
    for dx in (1, 2, 3):
        pl.semaphore_signal(barrier, inc=1, device_id=(mass_at(0, dx), r), device_id_type=MESH)
    for dy in (1, 2, 3):
        pl.semaphore_signal(barrier, inc=1, device_id=(m, y_rep(dy, c)), device_id_type=MESH)
    pl.semaphore_signal(barrier, inc=1, device_id=(m, y * 2 + 1 - c), device_id_type=MESH)

    def unit(values):
        widened = values.astype(jnp.float32)
        inverse = lax.rsqrt(jnp.mean(widened * widened, axis=-1, keepdims=True) + epsilon)
        return widened * inverse

    load_q.wait()

    def own_rows(i):
        two = unit(q_in[pl.ds(pl.multiple_of(i * 16, 16), 16), :])
        for b in (0, 1):
            u = two[b * 8 : b * 8 + 8]
            for p in (0, 1):
                halves = [u[:, p * HALF + h * QUARTER : p * HALF + (h + 1) * QUARTER] for h in (0, 1)]
                at = pl.ds(pl.multiple_of((i * 2 + b) * SLOT, SLOT), SLOT)
                chunk[0, p, at, :] = jnp.concatenate(halves, axis=0).astype(jnp.bfloat16)

    repeat(8, own_rows, False)

    lane_block = lax.broadcasted_iota(jnp.int32, (1, 256), 1) // SLOT
    shard_id = lax.broadcasted_iota(jnp.int32, (64, 256), 0)
    shard_id = shard_id // 8 * NX + shard_id % NX
    hit = jnp.zeros((64, 256), jnp.float32)
    for v in range(TOPW):
        named = jnp.zeros((1, 256), jnp.int32)
        for b in range(BLOCKS):
            named = jnp.where(lane_block == b, w_ref[v, b], named)
        hit = jnp.where(shard_id == named, 1.0, hit)
    before = lax.broadcasted_iota(jnp.int32, (256, 256), 0)
    after = lax.broadcasted_iota(jnp.int32, (256, 256), 1) // SLOT
    earlier = jnp.where((before // SLOT < after) & (before % SLOT == 0), 1.0, 0.0).astype(jnp.bfloat16)
    count = jnp.dot(hit.astype(jnp.bfloat16), earlier, preferred_element_type=jnp.float32)
    code = jnp.where(hit > 0.5, count, -1.0)
    for plane in range(NZ):
        code_own[plane] = code[plane * 8 : plane * 8 + 8]

    pl.semaphore_wait(barrier, 13)

    codes = {}
    for dz, dp, k in CODES:
        codes[k] = remote(
            code_own.at[(z + dp * sign + NZ) % NZ], code_in.at[k], cs.at[k], cr.at[k], (mass_at(dz, 0), r)
        )
        codes[k].start()

    ring = []
    for n, (s, a, b, p) in enumerate(PIECES):
        ring.append(remote(chunk.at[a, p], chunk.at[b, p], zs.at[n], zr.at[n], (mass_at(s, 0), r)))
    ring[0].start()

    load_l.wait()

    def own_entries(i):
        at = pl.multiple_of(i * 16, 16)
        lib[pl.ds(pl.multiple_of(r * ENTRIES + at, 16), 16), :] = unit(l_in[pl.ds(at, 16), :]).astype(jnp.bfloat16)

    repeat(ENTRIES // 16, own_entries, False)
    ring[1].start()

    def entries(rep, part=None):
        first, size = (0, ENTRIES) if part is None else (part * (ENTRIES // 2), ENTRIES // 2)
        return lib.at[pl.ds(pl.multiple_of(rep * ENTRIES + first, 16), size)]

    def along_y(n, rep, dy, part=None):
        return remote(entries(rep, part), entries(rep, part), ys.at[n], yr.at[n], (m, y_rep(dy, c)))

    def to_sibling(n, rep):
        return remote(entries(rep), entries(rep), ks.at[n], kr.at[n], (m, y * 2 + 1 - c))

    lib_y = [
        along_y(0, r, 1, 0),
        along_y(1, r, -1, 1),
        along_y(2, r, 1, 1),
        along_y(3, r, -1, 0),
        along_y(4, y_rep(-1, c), 1, 0),
        along_y(5, y_rep(1, c), -1, 1),
    ]
    lib_c = [to_sibling(n, y_rep(dy, c)) for n, dy in enumerate((0, -1, 1, 2))]
    lib_y[0].start()
    lib_y[1].start()
    lib_c[0].start()

    diagonal = lax.broadcasted_iota(jnp.int32, (SLOT, 256), 1) % SLOT == lax.broadcasted_iota(jnp.int32, (SLOT, 256), 0)

    def pick(k, p, held):
        parts = []
        for d in range(NX):
            at = pl.ds((x + d) % NX, 1)
            line = code_own[z, at, :] if k == 0 else code_in[k, at, :]
            for slot in range(CAP):
                parts.append(jnp.where(diagonal & (line == float(slot)), 1.0, 0.0))
        select = jnp.concatenate(parts, axis=0).astype(jnp.bfloat16)
        for t in range(QUARTER // 256):
            at = pl.ds(t * 256, 256)
            out = jnp.dot(select, chunk[held, p, :, at], preferred_element_type=jnp.float32).astype(jnp.bfloat16)
            for d in range(NX):
                part = out[d * UNIT : (d + 1) * UNIT]
                if d == 0 and k < 6:
                    arrived[k, p, 0, :, at] = part
                else:
                    packed[k, p, d, :, at] = part

    hops = {}
    for k in range(8):
        dz = {6: -1, 7: 1}.get(k, 0)
        for p in (0, 1):
            for d in range(NX):
                if d or k >= 6:
                    hops[k, p, d] = remote(
                        packed.at[k, p, d], arrived.at[k, p, d], xs.at[k, p, d], xr.at[k, p, d], (mass_at(dz, d), r)
                    )

    def send(k, p):
        for d in range(NX):
            if (k, p, d) in hops:
                hops[k, p, d].start()

    def unpack(k, pieces=(0, 1)):
        for p in pieces:
            for d in range(NX):
                if (k, p, d) in hops:
                    hops[k, p, d].wait_recv()
        for p in pieces:
            for j in range(NX * CAP // 2):
                two = []
                for s in (2 * j, 2 * j + 1):
                    at = pl.ds(s % CAP * SLOT, SLOT)
                    two.append(arrived[k, p, s // CAP, at, :].astype(jnp.float32))
                for h in (0, 1):
                    block = jnp.concatenate([v[h * 8 : h * 8 + 8] for v in two], axis=0).astype(jnp.bfloat16)
                    first = p * HALF + h * QUARTER
                    rows[k * SLOTS + j * 16 : k * SLOTS + j * 16 + 16, first : first + QUARTER] = block

    def score(group, groups, first, size, place, part=None):
        bins = slice(0, BINS) if part is None else slice(part * HALF, part * HALF + HALF)
        out = lax.dot_general(
            lib[pl.ds(pl.multiple_of(first, 128), size), bins],
            rows[group * 128 : (group + groups) * 128, bins],
            (((1,), (1,)), ((), ())),
            preferred_element_type=jnp.float32,
        )
        at = pl.ds(place // 8, size // 8)
        for g in range(groups):
            new = out[:, g * 128 : g * 128 + 128].reshape(size // 8, 8, 128)
            scores[group + g, at] = scores[group + g, at] + new if part else new

    returns = {}
    for k in range(8):
        for d in range(NX):
            if k or d:
                at = pl.ds(k * SLOTS + d * CAP * QB, CAP * QB)
                returns[k, d] = remote(
                    outgoing.at[at], incoming.at[m], rs.at[k, d], rr.at[k, d], (mass_at(OFFSET[k], NX - d), r)
                )

    def choose(group):
        end_rows(scores.at[group], best)
        outgoing[group * 128 : group * 128 + 128, :] = best[...].T

    def give_back(k):
        for d in range(NX):
            if k or d:
                returns[k, d].start()
            else:
                incoming[m] = outgoing[0 : CAP * QB, :]

    pick(0, 0, 0)
    send(0, 0)
    pick(0, 1, 0)
    send(0, 1)

    for b in range(BLOCKS):
        for v in range(TOPW):
            shard = w_ref[v, b]
            line = code_own[shard // NX, pl.ds(shard % NX, 1), :]
            slot_of[b, v] = jnp.broadcast_to(line[:, b * SLOT : b * SLOT + 1], (8, 128))

    def score_quarters(group, groups, which):
        for i in which:
            score(group, groups, (y + (0, NY - 1, 1, 2)[i]) % NY * 2 * ENTRIES, 2 * ENTRIES, i * 2 * ENTRIES)

    def score_all(group, part=None):
        repeat(2, lambda i: score(group, 1, i * (SHARD // 2), SHARD // 2, i * (SHARD // 2), part), False)

    for n in range(14):
        if n < 10:
            ring[n].wait_send()
        else:
            k, p = LAST[n][2], LAST[n][3]
            for d in range(NX):
                hops[k, p, d].wait_send()
        if n + 2 < 10:
            ring[n + 2].start()
        elif n + 2 < 14:
            send(LAST[n + 2][2], LAST[n + 2][3])
        if n < 10:
            ring[n].wait_recv()
            b, p = PIECES[n][2], PIECES[n][3]
            if p == 0:
                codes[b].wait_recv()
            pick(b, p, b)
            send(b, p)
            if b in (4, 5):
                if p == 0:
                    codes[b + 2].wait_recv()
                pick(b + 2, p, b)
        if n == 2:
            lib_y[2].start()
            lib_y[3].start()
            unpack(0)
        elif n == 3:
            unpack(1)
        elif n == 4:
            lib_y[0].wait_recv()
            lib_y[1].wait_recv()
            lib_y[4].start()
            lib_y[5].start()
        elif n == 5:
            unpack(2)
        elif n == 6:
            lib_y[2].wait_recv()
            lib_y[3].wait_recv()
            lib_c[1].start()
            lib_c[2].start()
            lib_c[0].wait_recv()
            score_quarters(0, 2, (0,))
        elif n == 7:
            unpack(3)
            lib_c[1].wait_recv()
            lib_c[2].wait_recv()
            score_quarters(0, 2, (1, 2))
            score_quarters(2, 1, (0, 1, 2))
        elif n == 8:
            unpack(4)
            for group in (0, 1, 2):
                begin_rows(scores.at[group])
        elif n == 9:
            lib_y[4].wait_recv()
            lib_y[5].wait_recv()
            lib_c[3].start()
            lib_c[3].wait_recv()
            score_quarters(0, 2, (3,))
            choose(0)
            choose(1)
        elif n == 10:
            unpack(5)
            score_quarters(2, 1, (3,))
            choose(2)
            score_all(3)
        elif n == 11:
            begin_rows(scores.at[3])
            choose(3)
            unpack(6)
            score_all(4)
        elif n == 12:
            begin_rows(scores.at[4])
            choose(4)
            unpack(7, (0,))
            score_all(5, 0)
    for k in range(6):
        give_back(k)
    unpack(7, (1,))
    score_all(5, 1)
    begin_rows(scores.at[5])
    choose(5)
    give_back(6)
    give_back(7)

    for k, d in returns:
        returns[k, d].wait_recv()

    def fetch(b):
        for v in range(TOPW):
            shard, slot = w_ref[v, b], slot_of[b, v]
            found = [incoming[shard, i * QB : i * QB + QB, :] for i in range(CAP)]
            found = jnp.where(slot < 0.5, found[0], jnp.where(slot < 1.5, found[1], found[2]))
            lists[v, pl.ds(pl.multiple_of(b * QB, QB), QB), :] = found

    repeat(BLOCKS, fetch, 4)
    for v in range(TOPW):
        lists[v] = lists[v].T
    sub = lax.broadcasted_iota(jnp.int32, (8, 128), 0) % TOPW

    def mix(i):
        line = [lists[v, pl.ds(i, 1), :] for v in range(TOPW)]
        mixed[i] = jnp.where(sub == 0, line[0], jnp.where(sub == 1, line[1], jnp.where(sub == 2, line[2], line[3])))

    repeat(K, mix, 16)
    across(mixed, 2)
    repeat(4, lambda i: fine(mixed, 0, 16, 2, i))
    across(mixed, 1)
    collect(mixed, best)
    o_ref[...] = best[...].T

    for copy in codes.values():
        copy.wait_send()
    for k in range(6):
        for p in (0, 1):
            for d in range(1, NX):
                hops[k, p, d].wait_send()
    for copy in lib_y + lib_c:
        copy.wait_send()
    for copy in returns.values():
        copy.wait_send()


def on_device(queries, library, windows):
    bf16, f32, dma = jnp.bfloat16, jnp.float32, pltpu.SemaphoreType.DMA
    scores = pl.pallas_call(
        kernel,
        out_shape=jax.ShapeDtypeStruct((BLOCKS * QB, K), f32),
        in_specs=[
            pl.BlockSpec(memory_space=pl.ANY),
            pl.BlockSpec(memory_space=pl.ANY),
            pl.BlockSpec(memory_space=pltpu.SMEM),
        ],
        out_specs=pl.BlockSpec(memory_space=pltpu.VMEM),
        scratch_shapes=[
            pltpu.VMEM((BLOCKS * QB, BINS), bf16),
            pltpu.VMEM((ENTRIES, BINS), bf16),
            pltpu.VMEM((6, 2, BLOCKS * SLOT, QUARTER), bf16),
            pltpu.VMEM((8, 2, NX, UNIT, QUARTER), bf16),
            pltpu.VMEM((8, 2, NX, UNIT, QUARTER), bf16),
            pltpu.VMEM((8 * SLOTS, BINS), bf16),
            pltpu.VMEM((SHARD, BINS), bf16),
            pltpu.VMEM((6, SHARD // 8, 8, 128), f32),
            pltpu.VMEM((128, 128), f32),
            pltpu.VMEM((8 * SLOTS, K), f32),
            pltpu.VMEM((NZ * NX, CAP * QB, K), f32),
            pltpu.VMEM((NZ, 8, 256), f32),
            pltpu.VMEM((8, 8, 256), f32),
            pltpu.VMEM((BLOCKS, TOPW, 8, 128), f32),
            pltpu.VMEM((TOPW, 128, K), f32),
            pltpu.VMEM((K, 8, 128), f32),
            dma((2,)),
            dma((10,)),
            dma((10,)),
            dma((8, 2, NX)),
            dma((8, 2, NX)),
            dma((8,)),
            dma((8,)),
            dma((6,)),
            dma((6,)),
            dma((4,)),
            dma((4,)),
            dma((8, NX)),
            dma((8, NX)),
        ],
        compiler_params=pltpu.CompilerParams(
            collective_id=0, has_side_effects=True, vmem_limit_bytes=60 * 2**20
        ),
    )(queries, library, windows.T)
    return scores * (1.0 / math.sqrt(BINS))


def solution(mesh):
    placed = (P(("mass", "rep"), None), P(("mass", "rep"), None), P(("mass", "rep"), None))
    return jax.shard_map(
        on_device, mesh=mesh, in_specs=placed, out_specs=P(("mass", "rep"), None), check_vma=False
    )
```

```python
import math

import jax
import jax.numpy as jnp
from jax import lax
from jax.experimental import pallas as pl
from jax.experimental.pallas import tpu as pltpu
from jax.sharding import PartitionSpec as P

MESH = pl.DeviceIdType.MESH
NZ, NX, NY = 8, 4, 4
BINS = 4096
HALF, QUARTER = BINS // 2, BINS // 4
QB = 8
BLOCKS = 16
TOPW = 4
CAP = 3
K = 128
ENTRIES = 192
SHARD = 1536
SLOT = 2 * QB
UNIT = CAP * SLOT
SLOTS = NX * CAP * QB
epsilon = 1e-06

OFFSET = (0, -1, 1, -2, 2, -3, 3, -4)
PIECES = [(s, a, b, p) for s, a, b in ((1, 0, 1), (-1, 0, 2), (1, 1, 3), (-1, 2, 4), (1, 3, 5)) for p in (0, 1)]
LAST = {10: (-1, 4, 6, 0), 11: (-1, 4, 6, 1), 12: (1, 5, 7, 0), 13: (1, 5, 7, 1)}
CODES = ((1, 1, 1), (-1, -1, 2), (2, 2, 3), (-2, -2, 4), (3, 3, 5), (-2, -3, 6), (3, 4, 7))


def at_index(v, i, axis):
    return lax.index_in_dim(v, i, axis, keepdims=False)


def paired(a, b, axis, up):
    hi, lo = jnp.maximum(a, b), jnp.minimum(a, b)
    return jnp.stack([lo, hi] if up else [hi, lo], axis=axis)


def clean(v, top, low, up=False):
    shape = v.shape
    s = top
    while s >= low:
        w = v.reshape((shape[0] // (2 * s), 2, s) + shape[1:])
        v = paired(at_index(w, 0, 1), at_index(w, 1, 1), 1, up).reshape(shape)
        s //= 2
    return v


def batcher(v):
    n = v.shape[0]
    shape = v.shape
    p = 1
    while p < n:
        k = p
        while k >= 1:
            w = v.reshape((n // (2 * p), 2 * p // k, k) + shape[1:])
            if k == p:
                w = paired(at_index(w, 0, 1), at_index(w, 1, 1), 1, False)
            else:
                c = 2 * p // k
                mid = lax.slice_in_dim(w, 1, c - 1, axis=1)
                mid = mid.reshape((n // (2 * p), (c - 2) // 2, 2, k) + shape[1:])
                mid = paired(at_index(mid, 0, 2), at_index(mid, 1, 2), 2, False)
                mid = mid.reshape((n // (2 * p), c - 2, k) + shape[1:])
                w = jnp.concatenate([lax.slice_in_dim(w, 0, 1, axis=1), mid, lax.slice_in_dim(w, c - 1, c, axis=1)], axis=1)
            v = w.reshape(shape)
            k //= 2
        p *= 2
    return v


def backwards(v):
    n = v.shape[0]
    return jnp.concatenate([lax.slice_in_dim(v, n - 1 - i, n - i, axis=0) for i in range(n)], axis=0)


def repeat(count, body, unroll=True):
    def step(i, carry):
        body(i)
        return carry
    lax.fori_loop(0, count, step, 0, unroll=unroll)


def coarse(ref, base, n, top, low, i, width, up=False):
    v = jnp.stack([ref[pl.ds(base + n * j + i, width)] for j in range(8)], axis=0)
    v = clean(v, top, low, up)
    for j in range(8):
        ref[pl.ds(base + n * j + i, width)] = at_index(v, j, 0)


def fine(ref, base, n, groups, i, up=False):
    at = pl.ds(base + i * n * groups, n * groups)
    ref[at] = clean(ref[at], n // 2, 1, up)


def across(ref, shift):
    def body(i):
        i = i * 4
        a = jnp.stack([ref[pl.ds(16 * j + i, 4)] for j in range(8)], axis=0)
        r = jnp.stack([ref[pl.ds(16 * j + 12 - i, 4)] for j in range(8)], axis=0)
        flat = (32, 8, 128)
        ra = backwards(r.reshape(flat))
        rr = backwards(a.reshape(flat))
        a = jnp.maximum(a.reshape(flat), pltpu.roll(ra, shift, 1)).reshape(8, 4, 8, 128)
        r = jnp.maximum(r.reshape(flat), pltpu.roll(rr, shift, 1)).reshape(8, 4, 8, 128)
        a, r = clean(a, 4, 1), clean(r, 4, 1)
        for j in range(8):
            ref[pl.ds(16 * j + i, 4)] = at_index(a, j, 0)
            ref[pl.ds(16 * j + 12 - i, 4)] = at_index(r, j, 0)
    repeat(2, body)


def collect(ref, o_ref):
    own = lax.broadcasted_iota(jnp.int32, (1, 8, 8, 128), 1) == lax.broadcasted_iota(jnp.int32, (1, 8, 8, 128), 2)
    def body(g):
        v = clean(ref[pl.ds(g * 32, 32)], 8, 1).reshape(4, 8, 8, 128)
        o_ref[pl.ds(pl.multiple_of(g * 32, 32), 32), :] = jnp.sum(jnp.where(own, v, 0.0), axis=1).reshape(32, 128)
    repeat(4, body)


def sort_part(ref, c):
    def sort32(up):
        at = pl.ds(c * 64 + up * 32, 32)
        v = batcher(ref[at])
        ref[at] = backwards(v) if up else v

    for up in (0, 1):
        sort32(up)
    repeat(2, lambda i: coarse(ref, c * 64, 8, 4, 1, i * 4, 4, c > 0))
    repeat(2, lambda i: fine(ref, c * 64, 8, 4, i, c > 0))


def begin_rows(ref):
    for c in (0, 1):
        sort_part(ref, c)
    repeat(4, lambda i: coarse(ref, 0, 16, 4, 1, i * 4, 4))
    repeat(4, lambda i: fine(ref, 0, 16, 2, i))


def end_rows(ref, o_ref):
    def third(i):
        i = i * 4
        v = [ref[pl.ds(16 * j + i, 4)] for j in range(8)]
        for j in range(4, 8):
            v[j] = jnp.maximum(v[j], ref[pl.ds(16 * j + 64 + i, 4)])
        v = clean(jnp.stack(v, axis=0), 4, 1)
        for j in range(8):
            ref[pl.ds(16 * j + i, 4)] = at_index(v, j, 0)

    sort_part(ref, 2)
    repeat(4, third)
    repeat(4, lambda i: fine(ref, 0, 16, 2, i))
    for shift in (4, 2, 1):
        across(ref, shift)
        if shift != 1:
            repeat(4, lambda i: fine(ref, 0, 16, 2, i))
    collect(ref, o_ref)


def kernel(
    q_hbm, l_hbm, w_ref, o_ref,
    q_in, l_in, chunk, packed, arrived, rows, lib, scores, best, outgoing, incoming, code_own, code_in, slot_of, lists, mixed,
    load_sem, zs, zr, xs, xr, cs, cr, ys, yr, ks, kr, rs, rr,
):
    m, r = lax.axis_index("mass"), lax.axis_index("rep")
    z, x, y, c = m // NX, m % NX, r // 2, r % 2
    sign = 2 * c - 1

    def mass_at(dz, dx):
        return (z + dz * sign + NZ) % NZ * NX + (x + dx) % NX

    def remote(src, dst, send, recv, device):
        return pltpu.make_async_remote_copy(
            src_ref=src, dst_ref=dst, send_sem=send, recv_sem=recv, device_id=device, device_id_type=MESH
        )

    def y_rep(dy, core):
        return (y + dy * sign + NY) % NY * 2 + core

    load_q = pltpu.make_async_copy(q_hbm, q_in, load_sem.at[0])
    load_l = pltpu.make_async_copy(l_hbm, l_in, load_sem.at[1])
    load_q.start()
    load_l.start()

    barrier = pltpu.get_barrier_semaphore()

    for dz in (1, 2, 3, 5, 6, 7):
        pl.semaphore_signal(barrier, inc=1, device_id=((z + dz) % NZ * NX + x, r), device_id_type=MESH)
    for dx in (1, 2, 3):
        pl.semaphore_signal(barrier, inc=1, device_id=(mass_at(0, dx), r), device_id_type=MESH)
    for dy in (1, 3):
        pl.semaphore_signal(barrier, inc=1, device_id=(m, y_rep(dy, c)), device_id_type=MESH)
    pl.semaphore_signal(barrier, inc=1, device_id=(m, y * 2 + 1 - c), device_id_type=MESH)

    def unit(values):
        widened = values.astype(jnp.float32)
        inverse = lax.rsqrt(jnp.mean(widened * widened, axis=-1, keepdims=True) + epsilon)
        return widened * inverse

    load_q.wait()

    def own_rows(i):
        two = unit(q_in[pl.ds(pl.multiple_of(i * 16, 16), 16), :])
        for b in (0, 1):
            u = two[b * 8 : b * 8 + 8]
            for p in (0, 1):
                halves = [u[:, p * HALF + h * QUARTER : p * HALF + (h + 1) * QUARTER] for h in (0, 1)]
                at = pl.ds(pl.multiple_of((i * 2 + b) * SLOT, SLOT), SLOT)
                chunk[0, p, at, :] = jnp.concatenate(halves, axis=0).astype(jnp.bfloat16)

    repeat(8, own_rows, False)

    lane_block = lax.broadcasted_iota(jnp.int32, (1, 256), 1) // SLOT
    shard_id = lax.broadcasted_iota(jnp.int32, (64, 256), 0)
    shard_id = shard_id // 8 * NX + shard_id % NX
    hit = jnp.zeros((64, 256), jnp.float32)
    for v in range(TOPW):
        named = jnp.zeros((1, 256), jnp.int32)
        for b in range(BLOCKS):
            named = jnp.where(lane_block == b, w_ref[v, b], named)
        hit = jnp.where(shard_id == named, 1.0, hit)
    before = lax.broadcasted_iota(jnp.int32, (256, 256), 0)
    after = lax.broadcasted_iota(jnp.int32, (256, 256), 1) // SLOT
    earlier = jnp.where((before // SLOT < after) & (before % SLOT == 0), 1.0, 0.0).astype(jnp.bfloat16)
    count = jnp.dot(hit.astype(jnp.bfloat16), earlier, preferred_element_type=jnp.float32)
    code = jnp.where(hit > 0.5, count, -1.0)
    for plane in range(NZ):
        code_own[plane] = code[plane * 8 : plane * 8 + 8]

    pl.semaphore_wait(barrier, 12)

    codes = {}
    for dz, dp, k in CODES:
        codes[k] = remote(
            code_own.at[(z + dp * sign + NZ) % NZ], code_in.at[k], cs.at[k], cr.at[k], (mass_at(dz, 0), r)
        )
        codes[k].start()

    ring = []
    for n, (s, a, b, p) in enumerate(PIECES):
        ring.append(remote(chunk.at[a, p], chunk.at[b, p], zs.at[n], zr.at[n], (mass_at(s, 0), r)))
    ring[0].start()

    load_l.wait()

    def own_entries(i):
        at = pl.multiple_of(i * 16, 16)
        lib[pl.ds(pl.multiple_of(r * ENTRIES + at, 16), 16), :] = unit(l_in[pl.ds(at, 16), :]).astype(jnp.bfloat16)

    repeat(ENTRIES // 16, own_entries, False)
    ring[1].start()

    def entries(rep, part=None):
        first, size = (0, ENTRIES) if part is None else (part * (ENTRIES // 2), ENTRIES // 2)
        return lib.at[pl.ds(pl.multiple_of(rep * ENTRIES + first, 16), size)]

    def along_y(n, rep, dy, part=None):
        return remote(entries(rep, part), entries(rep, part), ys.at[n], yr.at[n], (m, y_rep(dy, c)))

    def to_sibling(n, rep):
        return remote(entries(rep), entries(rep), ks.at[n], kr.at[n], (m, y * 2 + 1 - c))

    lib_y = [
        along_y(0, r, 1, 0),
        along_y(1, r, -1, 1),
        along_y(2, r, 1, 1),
        along_y(3, r, -1, 0),
        along_y(4, y_rep(-1, c), 1, 0),
        along_y(5, y_rep(1, c), -1, 1),
    ]
    lib_c = [to_sibling(n, y_rep(dy, c)) for n, dy in enumerate((0, -1, 1, 2))]
    lib_y[0].start()
    lib_y[1].start()
    lib_c[0].start()

    diagonal = lax.broadcasted_iota(jnp.int32, (SLOT, 256), 1) % SLOT == lax.broadcasted_iota(jnp.int32, (SLOT, 256), 0)

    def pick(k, p, held):
        parts = []
        for d in range(NX):
            at = pl.ds((x + d) % NX, 1)
            line = code_own[z, at, :] if k == 0 else code_in[k, at, :]
            for slot in range(CAP):
                parts.append(jnp.where(diagonal & (line == float(slot)), 1.0, 0.0))
        select = jnp.concatenate(parts, axis=0).astype(jnp.bfloat16)
        for t in range(QUARTER // 256):
            at = pl.ds(t * 256, 256)
            out = jnp.dot(select, chunk[held, p, :, at], preferred_element_type=jnp.float32).astype(jnp.bfloat16)
            for d in range(NX):
                part = out[d * UNIT : (d + 1) * UNIT]
                if d == 0 and k < 6:
                    arrived[k, p, 0, :, at] = part
                else:
                    packed[k, p, d, :, at] = part

    hops = {}
    for k in range(8):
        dz = {6: -1, 7: 1}.get(k, 0)
        for p in (0, 1):
            for d in range(NX):
                if d or k >= 6:
                    hops[k, p, d] = remote(
                        packed.at[k, p, d], arrived.at[k, p, d], xs.at[k, p, d], xr.at[k, p, d], (mass_at(dz, d), r)
                    )

    def send(k, p):
        for d in range(NX):
            if (k, p, d) in hops:
                hops[k, p, d].start()

    def unpack(k, pieces=(0, 1)):
        for p in pieces:
            for d in range(NX):
                if (k, p, d) in hops:
                    hops[k, p, d].wait_recv()
        for p in pieces:
            for j in range(NX * CAP // 2):
                two = []
                for s in (2 * j, 2 * j + 1):
                    at = pl.ds(s % CAP * SLOT, SLOT)
                    two.append(arrived[k, p, s // CAP, at, :].astype(jnp.float32))
                for h in (0, 1):
                    block = jnp.concatenate([v[h * 8 : h * 8 + 8] for v in two], axis=0).astype(jnp.bfloat16)
                    first = p * HALF + h * QUARTER
                    rows[k * SLOTS + j * 16 : k * SLOTS + j * 16 + 16, first : first + QUARTER] = block

    def score(group, groups, first, size, place, part=None):
        bins = slice(0, BINS) if part is None else slice(part * HALF, part * HALF + HALF)
        out = lax.dot_general(
            lib[pl.ds(pl.multiple_of(first, 128), size), bins],
            rows[group * 128 : (group + groups) * 128, bins],
            (((1,), (1,)), ((), ())),
            preferred_element_type=jnp.float32,
        )
        at = pl.ds(place // 8, size // 8)
        for g in range(groups):
            new = out[:, g * 128 : g * 128 + 128].reshape(size // 8, 8, 128)
            scores[group + g, at] = scores[group + g, at] + new if part else new

    returns = {}
    for k in range(8):
        for d in range(NX):
            if k or d:
                at = pl.ds(k * SLOTS + d * CAP * QB, CAP * QB)
                returns[k, d] = remote(
                    outgoing.at[at], incoming.at[m], rs.at[k, d], rr.at[k, d], (mass_at(OFFSET[k], NX - d), r)
                )

    def choose(group):
        end_rows(scores.at[group], best)
        outgoing[group * 128 : group * 128 + 128, :] = best[...].T

    def give_back(k):
        for d in range(NX):
            if k or d:
                returns[k, d].start()
            else:
                incoming[m] = outgoing[0 : CAP * QB, :]

    pick(0, 0, 0)
    send(0, 0)
    pick(0, 1, 0)
    send(0, 1)

    for b in range(BLOCKS):
        for v in range(TOPW):
            shard = w_ref[v, b]
            line = code_own[shard // NX, pl.ds(shard % NX, 1), :]
            slot_of[b, v] = jnp.broadcast_to(line[:, b * SLOT : b * SLOT + 1], (8, 128))

    def score_quarters(group, groups, which):
        for i in which:
            score(group, groups, (y + (0, NY - 1, 1, 2)[i]) % NY * 2 * ENTRIES, 2 * ENTRIES, i * 2 * ENTRIES)

    def score_all(group, part=None):
        repeat(2, lambda i: score(group, 1, i * (SHARD // 2), SHARD // 2, i * (SHARD // 2), part), False)

    for n in range(12):
        if n < 10:
            ring[n].wait_send()
        else:
            k, p = LAST[n][2], LAST[n][3]
            for d in range(NX):
                hops[k, p, d].wait_send()
        if n + 2 < 10:
            ring[n + 2].start()
        elif n + 2 < 14:
            send(LAST[n + 2][2], LAST[n + 2][3])
        if n < 10:
            ring[n].wait_recv()
            b, p = PIECES[n][2], PIECES[n][3]
            if p == 0:
                codes[b].wait_recv()
            pick(b, p, b)
            send(b, p)
            if b in (4, 5):
                if p == 0:
                    codes[b + 2].wait_recv()
                pick(b + 2, p, b)
        if n == 2:
            lib_y[2].start()
            lib_y[3].start()
            unpack(0)
        elif n == 3:
            unpack(1)
        elif n == 4:
            lib_y[0].wait_recv()
            lib_y[1].wait_recv()
            lib_y[4].start()
            lib_y[5].start()
        elif n == 5:
            unpack(2)
        elif n == 6:
            lib_y[2].wait_recv()
            lib_y[3].wait_recv()
            lib_c[1].start()
            lib_c[2].start()
            lib_c[0].wait_recv()
            score_quarters(0, 2, (0,))
        elif n == 7:
            unpack(3)
            lib_c[1].wait_recv()
            lib_c[2].wait_recv()
            score_quarters(0, 2, (1, 2))
            score_quarters(2, 1, (0, 1, 2))
        elif n == 8:
            for group in (0, 1, 2):
                begin_rows(scores.at[group])
        elif n == 9:
            lib_y[4].wait_recv()
            lib_y[5].wait_recv()
            lib_c[3].start()
            unpack(4)
            lib_c[3].wait_recv()
            score_quarters(0, 2, (3,))
            choose(0)
            choose(1)
        elif n == 10:
            score_quarters(2, 1, (3,))
            choose(2)
            unpack(5)
            score_all(3)
        elif n == 11:
            begin_rows(scores.at[3])
            choose(3)
            unpack(6)
            score_all(4)
    begin_rows(scores.at[4])
    choose(4)
    unpack(7, (0,))
    score_all(5, 0)
    for k in range(6):
        give_back(k)
    unpack(7, (1,))
    score_all(5, 1)
    begin_rows(scores.at[5])
    choose(5)
    give_back(6)
    give_back(7)

    for k, d in returns:
        returns[k, d].wait_recv()

    def fetch(b):
        for v in range(TOPW):
            shard, slot = w_ref[v, b], slot_of[b, v]
            found = [incoming[shard, i * QB : i * QB + QB, :] for i in range(CAP)]
            found = jnp.where(slot < 0.5, found[0], jnp.where(slot < 1.5, found[1], found[2]))
            lists[v, pl.ds(pl.multiple_of(b * QB, QB), QB), :] = found

    repeat(BLOCKS, fetch, 4)
    for v in range(TOPW):
        lists[v] = lists[v].T
    sub = lax.broadcasted_iota(jnp.int32, (8, 128), 0) % TOPW

    def mix(i):
        line = [lists[v, pl.ds(i, 1), :] for v in range(TOPW)]
        mixed[i] = jnp.where(sub == 0, line[0], jnp.where(sub == 1, line[1], jnp.where(sub == 2, line[2], line[3])))

    repeat(K, mix, 16)
    across(mixed, 2)
    repeat(4, lambda i: fine(mixed, 0, 16, 2, i))
    across(mixed, 1)
    collect(mixed, best)
    o_ref[...] = best[...].T

    for copy in codes.values():
        copy.wait_send()
    for (k, _, _), copy in hops.items():
        if k != 6:
            copy.wait_send()
    for copy in lib_y + lib_c:
        copy.wait_send()
    for copy in returns.values():
        copy.wait_send()


def on_device(queries, library, windows):
    bf16, f32, dma = jnp.bfloat16, jnp.float32, pltpu.SemaphoreType.DMA
    scores = pl.pallas_call(
        kernel,
        out_shape=jax.ShapeDtypeStruct((BLOCKS * QB, K), f32),
        in_specs=[
            pl.BlockSpec(memory_space=pl.ANY),
            pl.BlockSpec(memory_space=pl.ANY),
            pl.BlockSpec(memory_space=pltpu.SMEM),
        ],
        out_specs=pl.BlockSpec(memory_space=pltpu.VMEM),
        scratch_shapes=[
            pltpu.VMEM((BLOCKS * QB, BINS), bf16),
            pltpu.VMEM((ENTRIES, BINS), bf16),
            pltpu.VMEM((6, 2, BLOCKS * SLOT, QUARTER), bf16),
            pltpu.VMEM((8, 2, NX, UNIT, QUARTER), bf16),
            pltpu.VMEM((8, 2, NX, UNIT, QUARTER), bf16),
            pltpu.VMEM((8 * SLOTS, BINS), bf16),
            pltpu.VMEM((SHARD, BINS), bf16),
            pltpu.VMEM((6, SHARD // 8, 8, 128), f32),
            pltpu.VMEM((128, 128), f32),
            pltpu.VMEM((8 * SLOTS, K), f32),
            pltpu.VMEM((NZ * NX, CAP * QB, K), f32),
            pltpu.VMEM((NZ, 8, 256), f32),
            pltpu.VMEM((8, 8, 256), f32),
            pltpu.VMEM((BLOCKS, TOPW, 8, 128), f32),
            pltpu.VMEM((TOPW, 128, K), f32),
            pltpu.VMEM((K, 8, 128), f32),
            dma((2,)),
            dma((10,)),
            dma((10,)),
            dma((8, 2, NX)),
            dma((8, 2, NX)),
            dma((8,)),
            dma((8,)),
            dma((6,)),
            dma((6,)),
            dma((4,)),
            dma((4,)),
            dma((8, NX)),
            dma((8, NX)),
        ],
        compiler_params=pltpu.CompilerParams(
            collective_id=0, has_side_effects=True, vmem_limit_bytes=60 * 2**20
        ),
    )(queries, library, windows.T)
    return scores * (1.0 / math.sqrt(BINS))


def solution(mesh):
    placed = (P(("mass", "rep"), None), P(("mass", "rep"), None), P(("mass", "rep"), None))
    return jax.shard_map(
        on_device, mesh=mesh, in_specs=placed, out_specs=P(("mass", "rep"), None), check_vma=False
    )
```

```python
import math

import jax
import jax.numpy as jnp
from jax import lax
from jax.experimental import pallas as pl
from jax.experimental.pallas import tpu as pltpu
from jax.sharding import PartitionSpec as P

MESH = pl.DeviceIdType.MESH
NZ, NX, NY = 8, 4, 4
BINS = 4096
HALF, QUARTER = BINS // 2, BINS // 4
QB = 8
BLOCKS = 16
TOPW = 4
CAP = 3
K = 128
ENTRIES = 192
SHARD = 1536
SLOT = 2 * QB
UNIT = CAP * SLOT
SLOTS = NX * CAP * QB
epsilon = 1e-06

OFFSET = (0, -1, 1, -2, 2, -3, 3, -4)
PIECES = [(s, a, b, p) for s, a, b in ((1, 0, 1), (-1, 0, 2), (1, 1, 3), (-1, 2, 4), (1, 3, 5)) for p in (0, 1)]
LAST = {10: (-1, 4, 6, 0), 11: (-1, 4, 6, 1), 12: (1, 5, 7, 0), 13: (1, 5, 7, 1)}
CODES = ((1, 1, 1), (-1, -1, 2), (2, 2, 3), (-2, -2, 4), (3, 3, 5), (-2, -3, 6), (3, 4, 7))


def at_index(v, i, axis):
    return lax.index_in_dim(v, i, axis, keepdims=False)


def paired(a, b, axis, up):
    hi, lo = jnp.maximum(a, b), jnp.minimum(a, b)
    return jnp.stack([lo, hi] if up else [hi, lo], axis=axis)


def clean(v, top, low, up=False):
    shape = v.shape
    s = top
    while s >= low:
        w = v.reshape((shape[0] // (2 * s), 2, s) + shape[1:])
        v = paired(at_index(w, 0, 1), at_index(w, 1, 1), 1, up).reshape(shape)
        s //= 2
    return v


def batcher(v):
    n = v.shape[0]
    shape = v.shape
    p = 1
    while p < n:
        k = p
        while k >= 1:
            w = v.reshape((n // (2 * p), 2 * p // k, k) + shape[1:])
            if k == p:
                w = paired(at_index(w, 0, 1), at_index(w, 1, 1), 1, False)
            else:
                c = 2 * p // k
                mid = lax.slice_in_dim(w, 1, c - 1, axis=1)
                mid = mid.reshape((n // (2 * p), (c - 2) // 2, 2, k) + shape[1:])
                mid = paired(at_index(mid, 0, 2), at_index(mid, 1, 2), 2, False)
                mid = mid.reshape((n // (2 * p), c - 2, k) + shape[1:])
                w = jnp.concatenate([lax.slice_in_dim(w, 0, 1, axis=1), mid, lax.slice_in_dim(w, c - 1, c, axis=1)], axis=1)
            v = w.reshape(shape)
            k //= 2
        p *= 2
    return v


def backwards(v):
    n = v.shape[0]
    return jnp.concatenate([lax.slice_in_dim(v, n - 1 - i, n - i, axis=0) for i in range(n)], axis=0)


def repeat(count, body, unroll=True):
    def step(i, carry):
        body(i)
        return carry
    lax.fori_loop(0, count, step, 0, unroll=unroll)


def coarse(ref, base, n, top, low, i, width, up=False):
    v = jnp.stack([ref[pl.ds(base + n * j + i, width)] for j in range(8)], axis=0)
    v = clean(v, top, low, up)
    for j in range(8):
        ref[pl.ds(base + n * j + i, width)] = at_index(v, j, 0)


def fine(ref, base, n, groups, i, up=False):
    at = pl.ds(base + i * n * groups, n * groups)
    ref[at] = clean(ref[at], n // 2, 1, up)


def across(ref, shift):
    def body(i):
        i = i * 4
        a = jnp.stack([ref[pl.ds(16 * j + i, 4)] for j in range(8)], axis=0)
        r = jnp.stack([ref[pl.ds(16 * j + 12 - i, 4)] for j in range(8)], axis=0)
        flat = (32, 8, 128)
        ra = backwards(r.reshape(flat))
        rr = backwards(a.reshape(flat))
        a = jnp.maximum(a.reshape(flat), pltpu.roll(ra, shift, 1)).reshape(8, 4, 8, 128)
        r = jnp.maximum(r.reshape(flat), pltpu.roll(rr, shift, 1)).reshape(8, 4, 8, 128)
        a, r = clean(a, 4, 1), clean(r, 4, 1)
        for j in range(8):
            ref[pl.ds(16 * j + i, 4)] = at_index(a, j, 0)
            ref[pl.ds(16 * j + 12 - i, 4)] = at_index(r, j, 0)
    repeat(2, body)


def collect(ref, o_ref):
    own = lax.broadcasted_iota(jnp.int32, (1, 8, 8, 128), 1) == lax.broadcasted_iota(jnp.int32, (1, 8, 8, 128), 2)
    def body(g):
        v = clean(ref[pl.ds(g * 32, 32)], 8, 1).reshape(4, 8, 8, 128)
        o_ref[pl.ds(pl.multiple_of(g * 32, 32), 32), :] = jnp.sum(jnp.where(own, v, 0.0), axis=1).reshape(32, 128)
    repeat(4, body)


def sort_part(ref, c):
    def sort32(up):
        at = pl.ds(c * 64 + up * 32, 32)
        v = batcher(ref[at])
        ref[at] = backwards(v) if up else v

    for up in (0, 1):
        sort32(up)
    repeat(2, lambda i: coarse(ref, c * 64, 8, 4, 1, i * 4, 4, c > 0))
    repeat(2, lambda i: fine(ref, c * 64, 8, 4, i, c > 0))


def begin_rows(ref):
    for c in (0, 1):
        sort_part(ref, c)
    repeat(4, lambda i: coarse(ref, 0, 16, 4, 1, i * 4, 4))
    repeat(4, lambda i: fine(ref, 0, 16, 2, i))


def end_rows(ref, o_ref):
    def third(i):
        i = i * 4
        v = [ref[pl.ds(16 * j + i, 4)] for j in range(8)]
        for j in range(4, 8):
            v[j] = jnp.maximum(v[j], ref[pl.ds(16 * j + 64 + i, 4)])
        v = clean(jnp.stack(v, axis=0), 4, 1)
        for j in range(8):
            ref[pl.ds(16 * j + i, 4)] = at_index(v, j, 0)

    sort_part(ref, 2)
    repeat(4, third)
    repeat(4, lambda i: fine(ref, 0, 16, 2, i))
    for shift in (4, 2, 1):
        across(ref, shift)
        if shift != 1:
            repeat(4, lambda i: fine(ref, 0, 16, 2, i))
    collect(ref, o_ref)


def kernel(
    q_hbm, l_hbm, w_ref, o_ref,
    q_in, l_in, chunk, packed, arrived, rows, lib, scores, best, outgoing, incoming, code_own, code_in, slot_of, lists, mixed,
    load_sem, zs, zr, xs, xr, cs, cr, ys, yr, ks, kr, rs, rr,
):
    m, r = lax.axis_index("mass"), lax.axis_index("rep")
    z, x, y, c = m // NX, m % NX, r // 2, r % 2
    sign = 2 * c - 1

    def mass_at(dz, dx):
        return (z + dz * sign + NZ) % NZ * NX + (x + dx) % NX

    def remote(src, dst, send, recv, device):
        return pltpu.make_async_remote_copy(
            src_ref=src, dst_ref=dst, send_sem=send, recv_sem=recv, device_id=device, device_id_type=MESH
        )

    def y_rep(dy, core):
        return (y + dy * sign + NY) % NY * 2 + core

    load_q = pltpu.make_async_copy(q_hbm, q_in, load_sem.at[0])
    load_l = pltpu.make_async_copy(l_hbm, l_in, load_sem.at[1])
    load_q.start()
    load_l.start()

    barrier = pltpu.get_barrier_semaphore()

    for dz in (1, 2, 3, 5, 6, 7):
        pl.semaphore_signal(barrier, inc=1, device_id=((z + dz) % NZ * NX + x, r), device_id_type=MESH)
    for dx in (1, 2, 3):
        pl.semaphore_signal(barrier, inc=1, device_id=(mass_at(0, dx), r), device_id_type=MESH)
    for dy in (1, 2, 3):
        pl.semaphore_signal(barrier, inc=1, device_id=(m, y_rep(dy, c)), device_id_type=MESH)
    pl.semaphore_signal(barrier, inc=1, device_id=(m, y * 2 + 1 - c), device_id_type=MESH)

    def unit(values):
        widened = values.astype(jnp.float32)
        inverse = lax.rsqrt(jnp.mean(widened * widened, axis=-1, keepdims=True) + epsilon)
        return widened * inverse

    load_q.wait()

    def own_rows(i):
        two = unit(q_in[pl.ds(pl.multiple_of(i * 16, 16), 16), :])
        for b in (0, 1):
            u = two[b * 8 : b * 8 + 8]
            for p in (0, 1):
                halves = [u[:, p * HALF + h * QUARTER : p * HALF + (h + 1) * QUARTER] for h in (0, 1)]
                at = pl.ds(pl.multiple_of((i * 2 + b) * SLOT, SLOT), SLOT)
                chunk[0, p, at, :] = jnp.concatenate(halves, axis=0).astype(jnp.bfloat16)

    repeat(8, own_rows, False)

    lane_block = lax.broadcasted_iota(jnp.int32, (1, 256), 1) // SLOT
    shard_id = lax.broadcasted_iota(jnp.int32, (64, 256), 0)
    shard_id = shard_id // 8 * NX + shard_id % NX
    hit = jnp.zeros((64, 256), jnp.float32)
    for v in range(TOPW):
        named = jnp.zeros((1, 256), jnp.int32)
        for b in range(BLOCKS):
            named = jnp.where(lane_block == b, w_ref[v, b], named)
        hit = jnp.where(shard_id == named, 1.0, hit)
    before = lax.broadcasted_iota(jnp.int32, (256, 256), 0)
    after = lax.broadcasted_iota(jnp.int32, (256, 256), 1) // SLOT
    earlier = jnp.where((before // SLOT < after) & (before % SLOT == 0), 1.0, 0.0).astype(jnp.bfloat16)
    count = jnp.dot(hit.astype(jnp.bfloat16), earlier, preferred_element_type=jnp.float32)
    code = jnp.where(hit > 0.5, count, -1.0)
    for plane in range(NZ):
        code_own[plane] = code[plane * 8 : plane * 8 + 8]

    pl.semaphore_wait(barrier, 13)

    codes = {}
    for dz, dp, k in CODES:
        codes[k] = remote(
            code_own.at[(z + dp * sign + NZ) % NZ], code_in.at[k], cs.at[k], cr.at[k], (mass_at(dz, 0), r)
        )

    ring = []
    for n, (s, a, b, p) in enumerate(PIECES):
        ring.append(remote(chunk.at[a, p], chunk.at[b, p], zs.at[n], zr.at[n], (mass_at(s, 0), r)))
    ring[0].start()
    for copy in codes.values():
        copy.start()

    load_l.wait()

    def own_entries(i):
        at = pl.multiple_of(i * 16, 16)
        lib[pl.ds(pl.multiple_of(r * ENTRIES + at, 16), 16), :] = unit(l_in[pl.ds(at, 16), :]).astype(jnp.bfloat16)

    repeat(ENTRIES // 16, own_entries, False)
    ring[1].start()

    def entries(rep, part=None):
        first, size = (0, ENTRIES) if part is None else (part * (ENTRIES // 2), ENTRIES // 2)
        return lib.at[pl.ds(pl.multiple_of(rep * ENTRIES + first, 16), size)]

    def along_y(n, rep, dy, part=None):
        return remote(entries(rep, part), entries(rep, part), ys.at[n], yr.at[n], (m, y_rep(dy, c)))

    def to_sibling(n, rep):
        return remote(entries(rep), entries(rep), ks.at[n], kr.at[n], (m, y * 2 + 1 - c))

    lib_y = [
        along_y(0, r, 1, 0),
        along_y(1, r, -1, 1),
        along_y(2, r, 1, 1),
        along_y(3, r, -1, 0),
        along_y(4, y_rep(-1, c), 1, 0),
        along_y(5, y_rep(1, c), -1, 1),
    ]
    lib_c = [to_sibling(n, y_rep(dy, c)) for n, dy in enumerate((0, -1, 1, 2))]
    lib_y[0].start()
    lib_y[1].start()
    lib_c[0].start()

    diagonal = lax.broadcasted_iota(jnp.int32, (SLOT, 256), 1) % SLOT == lax.broadcasted_iota(jnp.int32, (SLOT, 256), 0)

    def pick(k, p, held):
        parts = []
        for d in range(NX):
            at = pl.ds((x + d) % NX, 1)
            line = code_own[z, at, :] if k == 0 else code_in[k, at, :]
            for slot in range(CAP):
                parts.append(jnp.where(diagonal & (line == float(slot)), 1.0, 0.0))
        select = jnp.concatenate(parts, axis=0).astype(jnp.bfloat16)
        for t in range(QUARTER // 256):
            at = pl.ds(t * 256, 256)
            out = jnp.dot(select, chunk[held, p, :, at], preferred_element_type=jnp.float32).astype(jnp.bfloat16)
            for d in range(NX):
                part = out[d * UNIT : (d + 1) * UNIT]
                if d == 0 and k < 6:
                    arrived[k, p, 0, :, at] = part
                else:
                    packed[k, p, d, :, at] = part

    hops = {}
    for k in range(8):
        dz = {6: -1, 7: 1}.get(k, 0)
        for p in (0, 1):
            for d in range(NX):
                if d or k >= 6:
                    hops[k, p, d] = remote(
                        packed.at[k, p, d], arrived.at[k, p, d], xs.at[k, p, d], xr.at[k, p, d], (mass_at(dz, d), r)
                    )

    def send(k, p):
        for d in range(NX):
            if (k, p, d) in hops:
                hops[k, p, d].start()

    def unpack(k, pieces=(0, 1)):
        for p in pieces:
            for d in range(NX):
                if (k, p, d) in hops:
                    hops[k, p, d].wait_recv()
        for p in pieces:
            for j in range(NX * CAP // 2):
                two = []
                for s in (2 * j, 2 * j + 1):
                    at = pl.ds(s % CAP * SLOT, SLOT)
                    two.append(arrived[k, p, s // CAP, at, :].astype(jnp.float32))
                for h in (0, 1):
                    block = jnp.concatenate([v[h * 8 : h * 8 + 8] for v in two], axis=0).astype(jnp.bfloat16)
                    first = p * HALF + h * QUARTER
                    rows[k * SLOTS + j * 16 : k * SLOTS + j * 16 + 16, first : first + QUARTER] = block

    def score(group, groups, first, size, place, part=None):
        bins = slice(0, BINS) if part is None else slice(part * HALF, part * HALF + HALF)
        out = lax.dot_general(
            lib[pl.ds(pl.multiple_of(first, 128), size), bins],
            rows[group * 128 : (group + groups) * 128, bins],
            (((1,), (1,)), ((), ())),
            preferred_element_type=jnp.float32,
        )
        at = pl.ds(place // 8, size // 8)
        for g in range(groups):
            new = out[:, g * 128 : g * 128 + 128].reshape(size // 8, 8, 128)
            scores[group + g, at] = scores[group + g, at] + new if part else new

    returns = {}
    for k in range(8):
        for d in range(NX):
            if k or d:
                at = pl.ds(k * SLOTS + d * CAP * QB, CAP * QB)
                returns[k, d] = remote(
                    outgoing.at[at], incoming.at[m], rs.at[k, d], rr.at[k, d], (mass_at(OFFSET[k], NX - d), r)
                )

    def choose(group):
        end_rows(scores.at[group], best)
        outgoing[group * 128 : group * 128 + 128, :] = best[...].T

    def give_back(k):
        for d in range(NX):
            if k or d:
                returns[k, d].start()
            else:
                incoming[m] = outgoing[0 : CAP * QB, :]

    pick(0, 0, 0)
    send(0, 0)
    pick(0, 1, 0)
    send(0, 1)

    for b in range(BLOCKS):
        for v in range(TOPW):
            shard = w_ref[v, b]
            line = code_own[shard // NX, pl.ds(shard % NX, 1), :]
            slot_of[b, v] = jnp.broadcast_to(line[:, b * SLOT : b * SLOT + 1], (8, 128))

    def score_quarters(group, groups, which):
        for i in which:
            score(group, groups, (y + (0, NY - 1, 1, 2)[i]) % NY * 2 * ENTRIES, 2 * ENTRIES, i * 2 * ENTRIES)

    def score_all(group, part=None):
        repeat(2, lambda i: score(group, 1, i * (SHARD // 2), SHARD // 2, i * (SHARD // 2), part), False)

    for n in range(12):
        if n < 10:
            ring[n].wait_send()
        else:
            k, p = LAST[n][2], LAST[n][3]
            for d in range(NX):
                hops[k, p, d].wait_send()
        if n + 2 < 10:
            ring[n + 2].start()
        elif n + 2 < 14:
            send(LAST[n + 2][2], LAST[n + 2][3])
        if n < 10:
            ring[n].wait_recv()
            b, p = PIECES[n][2], PIECES[n][3]
            if p == 0:
                codes[b].wait_recv()
            pick(b, p, b)
            send(b, p)
            if b in (4, 5):
                if p == 0:
                    codes[b + 2].wait_recv()
                pick(b + 2, p, b)
        if n == 2:
            lib_y[2].start()
            lib_y[3].start()
            unpack(0)
        elif n == 3:
            unpack(1)
        elif n == 4:
            lib_y[0].wait_recv()
            lib_y[1].wait_recv()
            lib_y[4].start()
            lib_y[5].start()
        elif n == 5:
            unpack(2)
        elif n == 6:
            lib_y[2].wait_recv()
            lib_y[3].wait_recv()
            lib_c[1].start()
            lib_c[2].start()
            lib_c[0].wait_recv()
            score_quarters(0, 2, (0,))
        elif n == 7:
            unpack(3)
            lib_c[1].wait_recv()
            lib_c[2].wait_recv()
            score_quarters(0, 2, (1, 2))
            score_quarters(2, 1, (0, 1, 2))
        elif n == 8:
            unpack(4)
            for group in (0, 1, 2):
                begin_rows(scores.at[group])
        elif n == 9:
            lib_y[4].wait_recv()
            lib_y[5].wait_recv()
            lib_c[3].start()
            lib_c[3].wait_recv()
            score_quarters(0, 2, (3,))
            choose(0)
            choose(1)
        elif n == 10:
            unpack(5)
            score_quarters(2, 1, (3,))
            choose(2)
            score_all(3)
        elif n == 11:
            begin_rows(scores.at[3])
            choose(3)
            unpack(6)
            score_all(4)
    begin_rows(scores.at[4])
    choose(4)
    unpack(7, (0,))
    score_all(5, 0)
    for k in range(6):
        give_back(k)
    unpack(7, (1,))
    score_all(5, 1)
    begin_rows(scores.at[5])
    choose(5)
    give_back(6)
    give_back(7)

    for k, d in returns:
        returns[k, d].wait_recv()

    def fetch(b):
        for v in range(TOPW):
            shard, slot = w_ref[v, b], slot_of[b, v]
            found = [incoming[shard, i * QB : i * QB + QB, :] for i in range(CAP)]
            found = jnp.where(slot < 0.5, found[0], jnp.where(slot < 1.5, found[1], found[2]))
            lists[v, pl.ds(pl.multiple_of(b * QB, QB), QB), :] = found

    repeat(BLOCKS, fetch, 4)
    for v in range(TOPW):
        lists[v] = lists[v].T
    sub = lax.broadcasted_iota(jnp.int32, (8, 128), 0) % TOPW

    def mix(i):
        line = [lists[v, pl.ds(i, 1), :] for v in range(TOPW)]
        mixed[i] = jnp.where(sub == 0, line[0], jnp.where(sub == 1, line[1], jnp.where(sub == 2, line[2], line[3])))

    repeat(K, mix, 16)
    across(mixed, 2)
    repeat(4, lambda i: fine(mixed, 0, 16, 2, i))
    across(mixed, 1)
    collect(mixed, best)
    o_ref[...] = best[...].T

    for copy in codes.values():
        copy.wait_send()
    for (k, _, _), copy in hops.items():
        if k != 6:
            copy.wait_send()
    for copy in lib_y + lib_c:
        copy.wait_send()
    for copy in returns.values():
        copy.wait_send()


def on_device(queries, library, windows):
    bf16, f32, dma = jnp.bfloat16, jnp.float32, pltpu.SemaphoreType.DMA
    scores = pl.pallas_call(
        kernel,
        out_shape=jax.ShapeDtypeStruct((BLOCKS * QB, K), f32),
        in_specs=[
            pl.BlockSpec(memory_space=pl.ANY),
            pl.BlockSpec(memory_space=pl.ANY),
            pl.BlockSpec(memory_space=pltpu.SMEM),
        ],
        out_specs=pl.BlockSpec(memory_space=pltpu.VMEM),
        scratch_shapes=[
            pltpu.VMEM((BLOCKS * QB, BINS), bf16),
            pltpu.VMEM((ENTRIES, BINS), bf16),
            pltpu.VMEM((6, 2, BLOCKS * SLOT, QUARTER), bf16),
            pltpu.VMEM((8, 2, NX, UNIT, QUARTER), bf16),
            pltpu.VMEM((8, 2, NX, UNIT, QUARTER), bf16),
            pltpu.VMEM((8 * SLOTS, BINS), bf16),
            pltpu.VMEM((SHARD, BINS), bf16),
            pltpu.VMEM((6, SHARD // 8, 8, 128), f32),
            pltpu.VMEM((128, 128), f32),
            pltpu.VMEM((8 * SLOTS, K), f32),
            pltpu.VMEM((NZ * NX, CAP * QB, K), f32),
            pltpu.VMEM((NZ, 8, 256), f32),
            pltpu.VMEM((8, 8, 256), f32),
            pltpu.VMEM((BLOCKS, TOPW, 8, 128), f32),
            pltpu.VMEM((TOPW, 128, K), f32),
            pltpu.VMEM((K, 8, 128), f32),
            dma((2,)),
            dma((10,)),
            dma((10,)),
            dma((8, 2, NX)),
            dma((8, 2, NX)),
            dma((8,)),
            dma((8,)),
            dma((6,)),
            dma((6,)),
            dma((4,)),
            dma((4,)),
            dma((8, NX)),
            dma((8, NX)),
        ],
        compiler_params=pltpu.CompilerParams(
            collective_id=0, has_side_effects=True, vmem_limit_bytes=60 * 2**20
        ),
    )(queries, library, windows.T)
    return scores * (1.0 / math.sqrt(BINS))


def solution(mesh):
    placed = (P(("mass", "rep"), None), P(("mass", "rep"), None), P(("mass", "rep"), None))
    return jax.shard_map(
        on_device, mesh=mesh, in_specs=placed, out_specs=P(("mass", "rep"), None), check_vma=False
    )
```
